32 devices in a mesh: lon: 16 (over z, y, core), lat: 2 (over x).
Axes of the slice: x: 2, y: 2, z: 4, core: 2. Of those that a mesh axis runs over, the one named last changes fastest.
Arguments:
- fields: bfloat16 [2, 12, 192, 192], P(None, 'lat', 'lon'), may hold values from -6 to 6
- cotangent: bfloat16 [2, 12, 192, 192], P(None, 'lat', 'lon'), may hold values from -6 to 6
- land_sea: int32 [12, 192], P('lat', 'lon'), may hold values 0 or 1
- orography: int32 [12, 192], P('lat', 'lon'), may hold values from 0 to 15
- land_vec: float32 [192], replicated, may hold values from -4 to 4
- orog_table: float32 [16, 192], replicated, may hold values from -4 to 4
- gain_attn: float32 [192], replicated, may hold values from 0.1 to 1.9
- w_qkv: bfloat16 [192, 576], replicated, may hold values from -0.4375 to 0.4375
- w_proj: bfloat16 [192, 192], replicated, may hold values from -0.4375 to 0.4375
- gain_mlp: float32 [192], replicated, may hold values from 0.1 to 1.9
- w_in: bfloat16 [192, 768], replicated, may hold values from -0.4375 to 0.4375
- w_out: bfloat16 [768, 192], replicated, may hold values from -0.21875 to 0.21875
- gain_merge: float32 [768], replicated, may hold values from 0.1 to 1.9
- w_merge: bfloat16 [768, 384], replicated, may hold values from -0.21875 to 0.21875
- gain_coarse: float32 [384], replicated, may hold values from 0.1 to 1.9
- w_cqkv: bfloat16 [384, 1152], replicated, may hold values from -0.3125 to 0.3125
- w_cproj: bfloat16 [384, 384], replicated, may hold values from -0.3125 to 0.3125
- w_up: bfloat16 [384, 768], replicated, may hold values from -0.3125 to 0.3125
Outputs:
- prediction: bfloat16 [2, 12, 192, 192], P(None, 'lat', 'lon')
- grad_input: bfloat16 [2, 12, 192, 192], P(None, 'lat', 'lon')
- grad_qkv: float32 [192, 576], replicated
- grad_proj: float32 [192, 192], replicated
The draws below stay inside these ranges and needn't reach their ends.
All inputs are finite; a program needn't handle non-finite values. No bound on the sum of `land_sea` on one device may be relied on, other than what follows from the above.
Results may differ from the reference program's by a relative error of at most 0.013.
Values may be sent and summed in bfloat16 or wider, within the bound.
A program may use at most 64 MiB of HBM per device.

```python
import math
import jax
import jax.numpy as jnp
from jax import lax

HEADS_F = 6
HEADS_C = 12
LEVELS = 2
WLAT = 6
WLON = 12
OROG = 16
C = 192
CC = 384
HID = 768
NLAT = 12
NLON = 192


def with_ends(entries, own_key, smallest, largest):
    dims = entries.shape
    spot = [jax.random.randint(jax.random.fold_in(own_key, axis), (), 0, dims[axis]) for axis in range(len(dims))]
    entries = entries.at[tuple(spot)].set(smallest)
    longest = dims.index(max(dims))
    spot[longest] = (spot[longest] + 1) % dims[longest]
    return entries.at[tuple(spot)].set(largest)


def steps_of(stream_key, shape, split, smallest, largest):
    factor_of, own = 1.0, jax.random.fold_in(stream_key, 6)
    for position, blocks in split:
        heights = jnp.exp(jax.random.uniform(jax.random.fold_in(own, position), (blocks,), jnp.float32, smallest / len(split), largest / len(split)))
        factor_of = factor_of * jnp.repeat(heights, shape[position] // blocks).reshape([-1 if axis == position else 1 for axis in range(len(shape))])
    return factor_of


def noise(key, extent, width, limit, pieces=(), kind=jnp.bfloat16):
    factor_of = steps_of(key, extent, pieces, -0.22, 0.18) if pieces else 1.0
    values = jax.random.normal(key, extent, jnp.float32) * width * factor_of
    return jnp.minimum(jnp.maximum(values, -limit), limit).astype(kind)


def setup_inputs(seed: int = 0) -> dict:
    streams_of = jax.random.split(jax.random.key(seed), 19)
    return {
        "fields": noise(streams_of[0], (LEVELS, NLAT, NLON, C), 1.0, 6.0, ((1, 2), (2, 16))),
        "cotangent": noise(streams_of[1], (LEVELS, NLAT, NLON, C), 1.0, 6.0, ((1, 2), (2, 16))),
        "land_sea": with_ends((jax.random.randint(streams_of[2], (NLAT, NLON), 0, 3) < 1).astype(jnp.int32), jax.random.fold_in(streams_of[2], 1), 0, 1),
        "orography": with_ends(jax.random.randint(streams_of[3], (NLAT, NLON), 0, OROG), jax.random.fold_in(streams_of[3], 1), 0, OROG - 1).astype(jnp.int32),
        "land_vec": noise(streams_of[4], (C,), 1.0, 4.0, (), jnp.float32),
        "orog_table": noise(streams_of[5], (OROG, C), 1.0, 4.0, (), jnp.float32),
        "gain_attn": jnp.clip(1.0 + 0.18 * jax.random.normal(streams_of[6], (C,), jnp.float32), 0.1, 1.9),
        "w_qkv": noise(streams_of[7], (C, 3 * C), C ** -0.5, 0.4375),
        "w_proj": noise(streams_of[8], (C, C), C ** -0.5, 0.4375),
        "gain_mlp": jnp.clip(1.0 + 0.18 * jax.random.normal(streams_of[9], (C,), jnp.float32), 0.1, 1.9),
        "w_in": noise(streams_of[10], (C, HID), C ** -0.5, 0.4375),
        "w_out": noise(streams_of[11], (HID, C), HID ** -0.5, 0.21875),
        "gain_merge": jnp.clip(1.0 + 0.18 * jax.random.normal(streams_of[12], (4 * C,), jnp.float32), 0.1, 1.9),
        "w_merge": noise(streams_of[13], (4 * C, CC), (4 * C) ** -0.5, 0.21875),
        "gain_coarse": jnp.clip(1.0 + 0.18 * jax.random.normal(streams_of[14], (CC,), jnp.float32), 0.1, 1.9),
        "w_cqkv": noise(streams_of[15], (CC, 3 * CC), CC ** -0.5, 0.3125),
        "w_cproj": noise(streams_of[16], (CC, CC), CC ** -0.5, 0.3125),
        "w_up": noise(streams_of[17], (CC, 4 * C), CC ** -0.5, 0.3125),
    }


epsilon = 1e-05
gelu_coeff = 0.7978845608028654

def layer_norm(values, gain_vec):
    average = lax.optimization_barrier(jnp.mean(values, axis=-1, keepdims=True))
    centred = values - average
    spread = lax.optimization_barrier(jnp.mean(centred * centred, axis=-1, keepdims=True))
    return centred * lax.rsqrt(spread + epsilon) * gain_vec

def layer_norm_back(values, gain_vec, upstream):
    average = lax.optimization_barrier(jnp.mean(values, axis=-1, keepdims=True))
    centred = values - average
    spread = lax.optimization_barrier(jnp.mean(centred * centred, axis=-1, keepdims=True))
    inverse = lax.rsqrt(spread + epsilon)
    normal = centred * inverse
    scaled = upstream * gain_vec
    return inverse * (scaled - lax.optimization_barrier(jnp.mean(scaled, axis=-1, keepdims=True)) - normal * lax.optimization_barrier(jnp.mean(scaled * normal, axis=-1, keepdims=True)))

def gelu_tanh(values):
    inner = gelu_coeff * (values + 0.044715 * values * values * values)
    return 0.5 * values * (1.0 + jnp.tanh(inner))

def gelu_slope(values):
    inner = gelu_coeff * (values + 0.044715 * values * values * values)
    tangent = jnp.tanh(inner)
    return 0.5 * (1.0 + tangent) + 0.5 * values * (1.0 - tangent * tangent) * gelu_coeff * (1.0 + 3.0 * 0.044715 * values * values)

def embed(fields, land_sea, orography, land_vec, orog_table):
    classes = (orography[..., None] == jnp.arange(orog_table.shape[0], dtype=jnp.int32)).astype(jnp.float32)
    lookup = jnp.dot(classes, orog_table, precision=lax.Precision.HIGHEST)
    surface = land_sea.astype(jnp.float32)[..., None] * land_vec + lookup
    return fields.astype(jnp.float32) + surface[None]

def merge_cells(tensor):
    levels, lat_rows, lon_cols, feature = tensor.shape
    tensor = tensor.reshape(levels, lat_rows // 2, 2, lon_cols // 2, 2, feature).transpose(0, 1, 3, 2, 4, 5)
    return tensor.reshape(levels, lat_rows // 2, lon_cols // 2, 4 * feature)

def split_cells(tensor):
    levels, lat_rows, lon_cols, wide = tensor.shape
    tensor = tensor.reshape(levels, lat_rows, lon_cols, 2, 2, wide // 4).transpose(0, 1, 3, 2, 4, 5)
    return tensor.reshape(levels, lat_rows * 2, lon_cols * 2, wide // 4)

def to_windows(tensor, win_rows, win_cols):
    levels, lat_rows, lon_cols, feature = tensor.shape
    tensor = tensor.reshape(levels // 2, 2, lat_rows // win_rows, win_rows, lon_cols // win_cols, win_cols, feature)
    tensor = tensor.transpose(0, 2, 4, 1, 3, 5, 6)
    return tensor.reshape(-1, 2 * win_rows * win_cols, feature)

def from_windows(tensor, levels, lat_rows, lon_cols, win_rows, win_cols):
    feature = tensor.shape[-1]
    tensor = tensor.reshape(levels // 2, lat_rows // win_rows, lon_cols // win_cols, 2, win_rows, win_cols, feature)
    return tensor.transpose(0, 3, 1, 4, 2, 5, 6).reshape(levels, lat_rows, lon_cols, feature)

def to_bands(tensor, height):
    levels, lat_rows, lon_cols, feature = tensor.shape
    return tensor.reshape(levels, lat_rows // height, height, lon_cols, feature).transpose(1, 0, 2, 3, 4)

def from_bands(stacked):
    count, levels, height, lon_cols, feature = stacked.shape
    return stacked.transpose(1, 0, 2, 3, 4).reshape(levels, count * height, lon_cols, feature)

def fine_mask(first_band):
    row_ids = jnp.arange(2 * WLAT * WLON, dtype=jnp.int32) // WLON % WLAT
    region = jnp.logical_and(first_band, row_ids < WLAT // 2)
    return (region[:, None] == region[None, :])[None, None]

def split_heads(tensor, heads):
    return tensor.reshape(tensor.shape[0], tensor.shape[1], heads, -1)

def attend_probs(queries, keys_in, allowed, heads):
    query_heads = split_heads(queries, heads).astype(jnp.float32)
    key_heads = split_heads(keys_in, heads).astype(jnp.float32)
    scores = jnp.einsum('wqhd,wkhd->whqk', query_heads, key_heads) / math.sqrt(query_heads.shape[-1])
    if allowed is not None:
        scores = jnp.where(allowed, scores, -1e+30)
    top = lax.optimization_barrier(jnp.max(scores, axis=-1, keepdims=True))
    expon = jnp.exp(scores - top)
    return expon / lax.optimization_barrier(jnp.sum(expon, axis=-1, keepdims=True))

def attend(queries, keys_in, values, allowed, heads):
    probs = attend_probs(queries, keys_in, allowed, heads)
    soft_bf = lax.optimization_barrier(probs.astype(jnp.bfloat16)).astype(jnp.float32)
    value_heads = split_heads(values, heads).astype(jnp.float32)
    mixed = jnp.einsum('whqk,wkhd->wqhd', soft_bf, value_heads)
    return mixed.reshape(queries.shape[0], queries.shape[1], -1).astype(jnp.bfloat16)

def attend_back(queries, keys_in, values, allowed, heads, grad_out):
    probs = attend_probs(queries, keys_in, allowed, heads)
    soft_bf = lax.optimization_barrier(probs.astype(jnp.bfloat16)).astype(jnp.float32)
    query_heads = split_heads(queries, heads).astype(jnp.float32)
    key_heads = split_heads(keys_in, heads).astype(jnp.float32)
    value_heads = split_heads(values, heads).astype(jnp.float32)
    grad_heads = split_heads(grad_out, heads).astype(jnp.float32)
    root = math.sqrt(query_heads.shape[-1])
    grad_values = jnp.einsum('whqk,wqhd->wkhd', soft_bf, grad_heads)
    grad_soft = jnp.einsum('wqhd,wkhd->whqk', grad_heads, value_heads)
    grad_scores = probs * (grad_soft - lax.optimization_barrier(jnp.sum(grad_soft * probs, axis=-1, keepdims=True)))
    score_bf = lax.optimization_barrier(grad_scores.astype(jnp.bfloat16)).astype(jnp.float32)
    grad_queries = jnp.einsum('whqk,wkhd->wqhd', score_bf, key_heads) / root
    grad_keys = jnp.einsum('whqk,wqhd->wkhd', score_bf, query_heads) / root
    windows = queries.shape[0]
    return (grad_queries.reshape(windows, queries.shape[1], -1), grad_keys.reshape(windows, keys_in.shape[1], -1), grad_values.reshape(windows, keys_in.shape[1], -1))

def reference(fields, cotangent, land_sea, orography, land_vec, orog_table, gain_attn, w_qkv, w_proj, gain_mlp, w_in, w_out, gain_merge, w_merge, gain_coarse, w_cqkv, w_cproj, w_up):
    levels = fields.shape[0]
    channels = fields.shape[3]
    coarse = w_cproj.shape[0]
    half_rows = WLAT // 2
    half_cols = WLON // 2
    base_field = embed(fields, land_sea, orography, land_vec, orog_table)
    normed = layer_norm(base_field, gain_attn).astype(jnp.bfloat16)
    rolled = jnp.roll(normed, (half_rows, half_cols), axis=(1, 2))
    fine_qkv = jnp.dot(rolled, w_qkv, preferred_element_type=jnp.float32).astype(jnp.bfloat16)
    band_ids = jnp.arange(NLAT // WLAT, dtype=jnp.int32)

    def fine_forward(parts):
        band, index = parts
        windows = to_windows(band, WLAT, WLON)
        result = attend(windows[..., :channels], windows[..., channels:2 * channels], windows[..., 2 * channels:], fine_mask(index == 0), HEADS_F)
        return from_windows(result, levels, WLAT, NLON, WLAT, WLON)
    attended = from_bands(lax.map(fine_forward, (to_bands(fine_qkv, WLAT), band_ids)))
    restored = jnp.roll(attended, (-half_rows, -half_cols), axis=(1, 2))
    first_res = base_field + jnp.dot(restored, w_proj, preferred_element_type=jnp.float32)
    mlp_in = layer_norm(first_res, gain_mlp).astype(jnp.bfloat16)
    pre_act = jnp.dot(mlp_in, w_in, preferred_element_type=jnp.float32)
    active = gelu_tanh(pre_act).astype(jnp.bfloat16)
    second_res = first_res + jnp.dot(active, w_out, preferred_element_type=jnp.float32)
    merged = merge_cells(second_res)
    merge_in = layer_norm(merged, gain_merge).astype(jnp.bfloat16)
    coarse_base = jnp.dot(merge_in, w_merge, preferred_element_type=jnp.float32)
    coarse_norm = layer_norm(coarse_base, gain_coarse).astype(jnp.bfloat16)
    coarse_qkv = jnp.dot(coarse_norm, w_cqkv, preferred_element_type=jnp.float32).astype(jnp.bfloat16)
    coarse_cols = NLON // 2

    def coarse_forward(band):
        windows = to_windows(band, WLAT, WLON)
        result = attend(windows[..., :coarse], windows[..., coarse:2 * coarse], windows[..., 2 * coarse:], None, HEADS_C)
        return from_windows(result, levels, WLAT, coarse_cols, WLAT, WLON)
    coarse_out = from_bands(lax.map(coarse_forward, to_bands(coarse_qkv, WLAT)))
    coarse_next = coarse_base + jnp.dot(coarse_out, w_cproj, preferred_element_type=jnp.float32)
    upward = jnp.dot(coarse_next.astype(jnp.bfloat16), w_up, preferred_element_type=jnp.float32)
    final = second_res + split_cells(upward)
    prediction = final.astype(jnp.bfloat16)
    grad_up = merge_cells(cotangent)
    grad_cnext = jnp.dot(grad_up, w_up.T, preferred_element_type=jnp.float32)
    grad_cout = jnp.dot(grad_cnext.astype(jnp.bfloat16), w_cproj.T, preferred_element_type=jnp.float32).astype(jnp.bfloat16)

    def coarse_backward(parts):
        band, grads = parts
        windows = to_windows(band, WLAT, WLON)
        grad_q, grad_k, grad_v = attend_back(windows[..., :coarse], windows[..., coarse:2 * coarse], windows[..., 2 * coarse:], None, HEADS_C, to_windows(grads, WLAT, WLON))
        joined = jnp.concatenate([grad_q, grad_k, grad_v], axis=-1).astype(jnp.bfloat16)
        return from_windows(joined, levels, WLAT, coarse_cols, WLAT, WLON)
    grad_cqkv = from_bands(lax.map(coarse_backward, (to_bands(coarse_qkv, WLAT), to_bands(grad_cout, WLAT))))
    grad_cnorm = jnp.dot(grad_cqkv, w_cqkv.T, preferred_element_type=jnp.float32)
    grad_cbase = grad_cnext + layer_norm_back(coarse_base, gain_coarse, grad_cnorm)
    grad_merge_in = jnp.dot(grad_cbase.astype(jnp.bfloat16), w_merge.T, preferred_element_type=jnp.float32)
    grad_second = cotangent.astype(jnp.float32) + split_cells(layer_norm_back(merged, gain_merge, grad_merge_in))
    grad_active = jnp.dot(grad_second.astype(jnp.bfloat16), w_out.T, preferred_element_type=jnp.float32)
    grad_pre = (grad_active * gelu_slope(pre_act)).astype(jnp.bfloat16)
    grad_mlp_in = jnp.dot(grad_pre, w_in.T, preferred_element_type=jnp.float32)
    grad_first = grad_second + layer_norm_back(first_res, gain_mlp, grad_mlp_in)
    grad_first_bf = grad_first.astype(jnp.bfloat16)
    grad_proj = jnp.dot(restored.reshape(-1, channels).T, grad_first_bf.reshape(-1, channels), preferred_element_type=jnp.float32)
    grad_restored = jnp.dot(grad_first_bf, w_proj.T, preferred_element_type=jnp.float32).astype(jnp.bfloat16)
    grad_attended = jnp.roll(grad_restored, (half_rows, half_cols), axis=(1, 2))

    def fine_backward(parts):
        band, grads, index = parts
        windows = to_windows(band, WLAT, WLON)
        grad_q, grad_k, grad_v = attend_back(windows[..., :channels], windows[..., channels:2 * channels], windows[..., 2 * channels:], fine_mask(index == 0), HEADS_F, to_windows(grads, WLAT, WLON))
        joined = jnp.concatenate([grad_q, grad_k, grad_v], axis=-1).astype(jnp.bfloat16)
        return from_windows(joined, levels, WLAT, NLON, WLAT, WLON)
    grad_fqkv = from_bands(lax.map(fine_backward, (to_bands(fine_qkv, WLAT), to_bands(grad_attended, WLAT), band_ids)))
    grad_qkv = jnp.dot(rolled.reshape(-1, channels).T, grad_fqkv.reshape(-1, 3 * channels), preferred_element_type=jnp.float32)
    grad_rolled = jnp.dot(grad_fqkv, w_qkv.T, preferred_element_type=jnp.float32).astype(jnp.bfloat16)
    grad_normed = jnp.roll(grad_rolled, (-half_rows, -half_cols), axis=(1, 2))
    grad_base = grad_first + layer_norm_back(base_field, gain_attn, grad_normed.astype(jnp.float32))
    return (prediction, grad_base.astype(jnp.bfloat16), grad_qkv, grad_proj)
```

```python
import functools
import math

import jax
import jax.numpy as jnp
import numpy as np
from jax import lax
from jax.experimental import pallas as pl
from jax.experimental.pallas import tpu as pltpu
from jax.sharding import PartitionSpec as P

HEADS_F = 6
WLAT = 6
WLON = 12
PAD = 48
FINE = 4 * PAD
MESH = pl.DeviceIdType.MESH
F32 = jnp.float32
BF16 = jnp.bfloat16

epsilon = 1e-05
gelu_coeff = 0.7978845608028654


def layer_norm(values, gain_vec):
    average = jnp.mean(values, axis=-1, keepdims=True)
    centred = values - average
    spread = jnp.mean(centred * centred, axis=-1, keepdims=True)
    return centred * lax.rsqrt(spread + epsilon) * gain_vec


def layer_norm_back(values, gain_vec, upstream):
    average = jnp.mean(values, axis=-1, keepdims=True)
    centred = values - average
    spread = jnp.mean(centred * centred, axis=-1, keepdims=True)
    inverse = lax.rsqrt(spread + epsilon)
    normal = centred * inverse
    scaled = upstream * gain_vec
    return inverse * (
        scaled
        - jnp.mean(scaled, axis=-1, keepdims=True)
        - normal * jnp.mean(scaled * normal, axis=-1, keepdims=True)
    )


def gelu_tanh(values):
    inner = gelu_coeff * (values + 0.044715 * values * values * values)
    return 0.5 * values * (1.0 + jnp.tanh(inner))


def gelu_slope(values):
    inner = gelu_coeff * (values + 0.044715 * values * values * values)
    tangent = jnp.tanh(inner)
    return 0.5 * (1.0 + tangent) + 0.5 * values * (1.0 - tangent * tangent) * gelu_coeff * (
        1.0 + 3.0 * 0.044715 * values * values
    )


def orderings():
    to_parity = np.zeros((FINE, 2 * WLAT * WLON), np.float32)
    to_quadrant = np.zeros((FINE, FINE), np.float32)
    for level in range(2):
        for row in range(WLAT):
            for col in range(WLON):
                natural = (level * WLAT + row) * WLON + col
                parity = (row % 2 * 2 + col % 2) * PAD + (level * 3 + row // 2) * 6 + col // 2
                quadrant = (row // 3 * 2 + col // 6) * PAD + (level * 3 + row % 3) * 6 + col % 6
                to_parity[parity, natural] = 1
                to_quadrant[quadrant, parity] = 1
    eye = np.eye(FINE, dtype=np.float32)
    fold = np.zeros((PAD, FINE), np.float32)
    for group in range(4):
        fold[:, group * PAD : (group + 1) * PAD] = np.eye(PAD)
    return [
        jnp.asarray(m, BF16)
        for m in (to_parity, to_parity.T, to_quadrant, to_quadrant.T, eye, fold)
    ]

def dot(a, b):
    return jnp.dot(a, b, preferred_element_type=F32)

def dot_nt(a, b):
    return lax.dot_general(a, b, (((1,), (1,)), ((), ())), preferred_element_type=F32)

def iota(shape, axis):
    return lax.broadcasted_iota(jnp.int32, shape, axis)

def blocks(tensor):
    return [tensor[g * PAD : (g + 1) * PAD] for g in range(4)]

def wide_mean(parts):
    total = parts[0]
    for part in parts[1:]:
        total = total + part
    return jnp.sum(total, axis=-1, keepdims=True) * (1.0 / (4 * total.shape[-1]))

def flip(index, bit):
    return index + bit * (1 - 2 * (index // bit % 2))

def kernel(
    sizes,
    fields,
    cotangent,
    surface_in,
    table,
    gain_attn,
    w_qkv,
    w_proj,
    gain_mlp,
    w_in,
    w_out,
    gain_merge,
    w_merge,
    gain_coarse,
    w_cqkv,
    w_cproj,
    w_up,
    to_parity,
    to_natural,
    to_quadrant,
    from_quadrant,
    eye,
    fold,
    pred_out,
    gin_out,
    gqkv_out,
    gproj_out,
    norm_send,
    norm_win,
    att_win,
    att_back,
    kv,
    gkv_send,
    gkv_recv,
    gres_send,
    gres_win,
    groll_win,
    groll_back,
    probs_f,
    probs_c,
    reduce_send,
    reduce_recv,
    line_send,
    line_recv,
    gathered,
    send_sem,
    recv_sem,
):
    lat_size, lon_size, reduces = sizes
    i = lax.axis_index("lat")
    j = lax.axis_index("lon")

    def at(lat, lon):
        return (lax.rem(lon + lon_size, lon_size), lax.rem(lat + lat_size, lat_size))

    ahead = [at(i, j + 1), at(i + 1, j), at(i + 1, j + 1)]
    behind = [at(i, j - 1), at(i - 1, j), at(i - 1, j - 1)]
    group = [(flip(j, 1), i), (j, flip(i, 1)), (flip(j, 1), flip(i, 1))]
    greeted = ahead + behind + group
    plane, line = [], []
    if reduces:
        for d in range(1, 8):
            lat = flip(i, 1) if d & 4 else i
            lon = flip(j, 2) if d & 2 else j
            lon = flip(lon, 1) if d & 1 else lon
            plane.append((lon, lat))
        for d in range(1, 4):
            lon = flip(j, 8) if d & 2 else j
            lon = flip(lon, 4) if d & 1 else lon
            line.append((lon, i))
        greeted = greeted + plane + line
    barrier = pltpu.get_barrier_semaphore()
    for device in greeted:
        pl.semaphore_signal(barrier, inc=1, device_id=device, device_id_type=MESH)

    started = []

    def send(source, target, device):
        n = len(started)
        copy = pltpu.make_async_remote_copy(
            src_ref=source,
            dst_ref=target,
            send_sem=send_sem.at[n],
            recv_sem=recv_sem.at[n],
            device_id=device,
            device_id_type=MESH,
        )
        copy.start()
        started.append(copy)
        return copy

    def exchange(source, target, devices):
        return [send(source.at[s + 1], target.at[s + 1], devices[s]) for s in range(3)]

    def arrive(copies):
        for copy in copies:
            copy.wait_recv()

    def place(ref, tensor):
        for g, part in enumerate(blocks(tensor)):
            ref[g] = part

    def whole(ref):
        return jnp.concatenate([ref[g] for g in range(4)], axis=0)

    root = 1.0 / math.sqrt(32.0)
    channels = w_proj.shape[0]
    coarse = w_cproj.shape[0]

    classes = dot(to_parity[...], surface_in[...])
    surface = jnp.dot(classes, table[...], precision=lax.Precision.HIGHEST)
    base = dot(to_parity[...], fields[...]) + surface
    normed = layer_norm(base, gain_attn[...]).astype(BF16)
    place(norm_send, dot(to_quadrant[...], normed).astype(BF16))
    norm_win[0] = norm_send[0]
    pl.semaphore_wait(barrier, len(greeted))
    moves = exchange(norm_send, norm_win, ahead)

    cot = dot(to_parity[...], cotangent[...])
    cot_bf = blocks(cot.astype(BF16))
    grad_cnext = sum(
        dot_nt(cot_bf[g], w_up[:, g * channels : (g + 1) * channels]) for g in range(4)
    )
    grad_cout = dot_nt(grad_cnext.astype(BF16), w_cproj[...]).astype(BF16)
    key_ids = iota((FINE, FINE), 0)
    query_ids = iota((FINE, FINE), 1)
    edge = jnp.where(i == 0, 1, 0)
    same = (key_ids // (2 * PAD) - query_ids // (2 * PAD)) * edge == 0
    real = key_ids % PAD < 36
    fine_bias = jnp.where(jnp.logical_and(same, real), 0.0, -1e30)
    coarse_bias = jnp.where(real, 0.0, -1e30)
    head_f = iota((FINE, channels), 1) // 32

    arrive(moves)
    rolled = whole(norm_win)
    w_q = w_qkv[:, :channels]
    w_k = w_qkv[:, channels : 2 * channels]
    w_v = w_qkv[:, 2 * channels :]
    q = dot(rolled, w_q).astype(BF16)
    k = dot(rolled, w_k).astype(BF16)
    v = dot(rolled, w_v).astype(BF16)
    zero = jnp.zeros_like(q)
    v_turned = dot_nt(eye[...], v).astype(BF16)
    att_turned = []
    for h in range(HEADS_F):
        scores = dot_nt(jnp.where(head_f == h, k, zero), q) * root + fine_bias
        expon = jnp.exp(scores - jnp.max(scores, axis=0, keepdims=True))
        probs = expon * (1.0 / jnp.sum(expon, axis=0, keepdims=True))
        probs_f[h] = probs
        att_turned.append(dot(v_turned[32 * h : 32 * h + 32], probs.astype(BF16)))
    att = dot_nt(eye[...], jnp.concatenate(att_turned, axis=0).astype(BF16)).astype(BF16)

    place(att_win, att)
    att_back[0] = att_win[0]
    moves = exchange(att_win, att_back, behind)
    arrive(moves)
    restored = dot(from_quadrant[...], whole(att_back)).astype(BF16)

    first = base + dot(restored, w_proj[...])
    mlp_in = layer_norm(first, gain_mlp[...]).astype(BF16)
    pre = dot(mlp_in, w_in[...])
    second = first + dot(gelu_tanh(pre).astype(BF16), w_out[...])

    merged = blocks(second)
    gains = [gain_merge[:, g * channels : (g + 1) * channels] for g in range(4)]
    average = wide_mean(merged)
    centred = [part - average for part in merged]
    inverse = lax.rsqrt(wide_mean([part * part for part in centred]) + epsilon)
    normal = [part * inverse for part in centred]
    coarse_base = sum(
        dot((normal[g] * gains[g]).astype(BF16), w_merge[g * channels : (g + 1) * channels, :])
        for g in range(4)
    )
    coarse_norm = layer_norm(coarse_base, gain_coarse[...]).astype(BF16)
    kv[0] = dot(coarse_norm, w_cqkv[:, coarse:]).astype(BF16)
    moves = [send(kv.at[0], kv.at[s + 1], group[s]) for s in range(3)]
    cq = dot(coarse_norm, w_cqkv[:, :coarse]).astype(BF16)
    block_rows = iota((FINE, 128), 0) // PAD
    own_head = block_rows == iota((FINE, 128), 1) // 32
    own_turned = iota((128, FINE), 0) // 32 == iota((128, FINE), 1) // PAD

    def spread(part):
        tall = jnp.concatenate([part] * 4, axis=0)
        return jnp.where(own_head, tall, jnp.zeros_like(tall))

    spread_q = [spread(cq[:, 128 * g : 128 * g + 128]) for g in range(3)]
    spread_do = [spread(grad_cout[:, 128 * g : 128 * g + 128]) for g in range(3)]
    arrive(moves)

    keys = whole(kv.at[:, :, :coarse])
    values = whole(kv.at[:, :, coarse:])
    score_grads = []
    for g in range(3):
        lanes = slice(128 * g, 128 * g + 128)
        scores = dot_nt(keys[:, lanes], spread_q[g]) * root + coarse_bias
        expon = jnp.exp(scores - jnp.max(scores, axis=0, keepdims=True))
        probs = expon * (1.0 / jnp.sum(expon, axis=0, keepdims=True))
        probs_c[g] = probs.astype(BF16)
        soft_grad = dot_nt(values[:, lanes], spread_do[g])
        kept = jnp.sum(soft_grad * probs, axis=0, keepdims=True)
        score_grad = (probs * (soft_grad - kept)).astype(BF16)
        score_grads.append(score_grad)
        grad_v = dot(probs_c[g], spread_do[g])
        grad_k = dot(score_grad, spread_q[g]) * root
        for s in range(4):
            rows = slice(s * PAD, (s + 1) * PAD)
            gkv_send[s, :, 128 * g : 128 * g + 128] = grad_k[rows].astype(BF16)
            gkv_send[s, :, coarse + 128 * g : coarse + 128 * g + 128] = grad_v[rows].astype(BF16)
    moves = exchange(gkv_send, gkv_recv, group)

    grad_cqs, outs = [], []
    for g in range(3):
        lanes = slice(128 * g, 128 * g + 128)
        small = eye[:128, :128]
        turned = dot(dot_nt(small, keys[:, lanes]).astype(BF16), score_grads[g]) * root
        grad_cqs.append(dot_nt(fold[...], jnp.where(own_turned, turned, 0.0).astype(BF16)))
        turned = dot(dot_nt(small, values[:, lanes]).astype(BF16), probs_c[g])
        outs.append(dot_nt(fold[...], jnp.where(own_turned, turned, 0.0).astype(BF16)))
    coarse_out = jnp.concatenate(outs, axis=1).astype(BF16)
    coarse_next = (coarse_base + dot(coarse_out, w_cproj[...])).astype(BF16)
    upward = jnp.concatenate(
        [dot(coarse_next, w_up[:, g * channels : (g + 1) * channels]) for g in range(4)], axis=0
    )
    pred_out[...] = dot(to_natural[...], (second + upward).astype(BF16)).astype(BF16)
    grad_cq = jnp.concatenate(grad_cqs, axis=1).astype(BF16)
    grad_cnorm = dot_nt(grad_cq, w_cqkv[:, :coarse])

    arrive(moves)
    grad_kv = gkv_send[0].astype(F32)
    for s in range(1, 4):
        grad_kv = grad_kv + gkv_recv[s].astype(F32)
    grad_cnorm = grad_cnorm + dot_nt(grad_kv.astype(BF16), w_cqkv[:, coarse:])
    grad_cbase = grad_cnext + layer_norm_back(coarse_base, gain_coarse[...], grad_cnorm)
    grad_cbase = grad_cbase.astype(BF16)
    scaled = [
        dot_nt(grad_cbase, w_merge[g * channels : (g + 1) * channels, :]) * gains[g]
        for g in range(4)
    ]
    mean_scaled = wide_mean(scaled)
    mean_both = wide_mean([scaled[g] * normal[g] for g in range(4)])
    grad_merged = [
        inverse * (scaled[g] - mean_scaled - normal[g] * mean_both) for g in range(4)
    ]
    grad_second = cot + jnp.concatenate(grad_merged, axis=0)
    grad_active = dot_nt(grad_second.astype(BF16), w_out[...])
    grad_pre = (grad_active * gelu_slope(pre)).astype(BF16)
    grad_mlp_in = dot_nt(grad_pre, w_in[...])
    grad_first = grad_second + layer_norm_back(first, gain_mlp[...], grad_mlp_in)
    grad_first_bf = grad_first.astype(BF16)
    grad_restored = dot_nt(grad_first_bf, w_proj[...]).astype(BF16)
    place(gres_send, dot(to_quadrant[...], grad_restored).astype(BF16))
    gres_win[0] = gres_send[0]
    moves = exchange(gres_send, gres_win, ahead)
    grad_proj = dot(dot_nt(eye[...], restored).astype(BF16), grad_first_bf)
    k_turned = dot_nt(eye[...], k).astype(BF16)
    rolled_turned = dot_nt(eye[...], rolled).astype(BF16)
    arrive(moves)

    do = whole(gres_win)
    grad_v = jnp.zeros((FINE, channels), F32)
    grad_k = jnp.zeros((FINE, channels), F32)
    gq_turned = []
    for h in range(HEADS_F):
        mine = head_f == h
        probs = probs_f[h]
        soft_grad = dot_nt(jnp.where(mine, v, zero), do)
        kept = jnp.sum(soft_grad * probs, axis=0, keepdims=True)
        score_grad = (probs * (soft_grad - kept)).astype(BF16)
        grad_v = grad_v + dot(probs.astype(BF16), jnp.where(mine, do, zero))
        grad_k = grad_k + dot(score_grad, jnp.where(mine, q, zero))
        gq_turned.append(dot(k_turned[32 * h : 32 * h + 32], score_grad) * root)
    grad_q = dot_nt(eye[...], jnp.concatenate(gq_turned, axis=0).astype(BF16)).astype(BF16)
    grad_k = (grad_k * root).astype(BF16)
    grad_v = grad_v.astype(BF16)
    grad_rolled = dot_nt(grad_q, w_q) + dot_nt(grad_k, w_k) + dot_nt(grad_v, w_v)
    place(groll_win, grad_rolled.astype(BF16))
    groll_back[0] = groll_win[0]
    moves = exchange(groll_win, groll_back, behind)

    part_q = dot(rolled_turned, grad_q)
    part_k = dot(rolled_turned, grad_k)
    part_v = dot(rolled_turned, grad_v)
    if reduces:
        for g in range(4):
            rows = slice(g * PAD, (g + 1) * PAD)
            reduce_send[g, :, :channels] = part_q[rows].astype(BF16)
            reduce_send[g, :, channels:] = part_k[rows].astype(BF16)
            reduce_send[4 + g, :, :channels] = part_v[rows].astype(BF16)
            reduce_send[4 + g, :, channels:] = grad_proj[rows].astype(BF16)
        me = i * 4 + j % 4
        to_owner = [
            send(reduce_send.at[lat * 4 + lon % 4], reduce_recv.at[d], (lon, lat))
            for d, (lon, lat) in enumerate(plane)
        ]
    else:
        gqkv_out[:, :channels] = part_q
        gqkv_out[:, channels : 2 * channels] = part_k
        gqkv_out[:, 2 * channels :] = part_v
        gproj_out[...] = grad_proj

    arrive(moves)
    grad_normed = dot(from_quadrant[...], whole(groll_back))
    grad_base = grad_first + layer_norm_back(base, gain_attn[...], grad_normed)
    gin_out[...] = dot(to_natural[...], grad_base.astype(BF16)).astype(BF16)

    if reduces:
        arrive(to_owner)
        total = reduce_send[me].astype(F32)
        for d in range(7):
            total = total + reduce_recv[d].astype(F32)
        line_send[...] = total.astype(BF16)
        moves = [send(line_send, line_recv.at[d], line[d]) for d in range(3)]
        arrive(moves)
        total = (line_send[...].astype(F32) + line_recv[0].astype(F32)) + (
            line_recv[1].astype(F32) + line_recv[2].astype(F32)
        )
        gathered[me] = total.astype(BF16)
        moves = [send(gathered.at[me], gathered.at[me], device) for device in plane]
        arrive(moves)
        for g in range(4):
            rows = slice(g * PAD, (g + 1) * PAD)
            left = gathered[g].astype(F32)
            right = gathered[4 + g].astype(F32)
            gqkv_out[rows, : 2 * channels] = left
            gqkv_out[rows, 2 * channels :] = right[:, :channels]
            gproj_out[rows, :] = right[:, channels:]
    for copy in started:
        copy.wait_send()

def per_device(
    sizes,
    fields,
    cotangent,
    land_sea,
    orography,
    land_vec,
    orog_table,
    gain_attn,
    w_qkv,
    w_proj,
    gain_mlp,
    w_in,
    w_out,
    gain_merge,
    w_merge,
    gain_coarse,
    w_cqkv,
    w_cproj,
    w_up,
):
    reduces = sizes[2]
    channels = fields.shape[-1]
    coarse = w_cproj.shape[0]
    tokens = 2 * WLAT * WLON
    kinds = orog_table.shape[0]
    lanes = jnp.arange(128, dtype=jnp.int32)
    land = jnp.where(lanes == kinds, land_sea.reshape(-1, 1), 0)
    classes = jnp.where(lanes == orography.reshape(-1, 1), 1, land).astype(BF16)
    classes = jnp.concatenate([classes, classes], axis=0)
    table = jnp.concatenate(
        [orog_table, land_vec[None], jnp.zeros((127 - kinds, channels), F32)], axis=0
    )
    operands = [
        fields.reshape(tokens, channels),
        cotangent.reshape(tokens, channels),
        classes,
        table,
        gain_attn[None],
        w_qkv,
        w_proj,
        gain_mlp[None],
        w_in,
        w_out,
        gain_merge[None],
        w_merge,
        gain_coarse[None],
        w_cqkv,
        w_cproj,
        w_up,
        *orderings(),
    ]
    tile = pltpu.VMEM((4, PAD, channels), BF16)
    wide = pltpu.VMEM((4, PAD, 2 * coarse), BF16)
    prediction, grad_input, grad_qkv, grad_proj = pl.pallas_call(
        functools.partial(kernel, sizes),
        out_shape=(
            jax.ShapeDtypeStruct((tokens, channels), BF16),
            jax.ShapeDtypeStruct((tokens, channels), BF16),
            jax.ShapeDtypeStruct((channels, 3 * channels), F32),
            jax.ShapeDtypeStruct((channels, channels), F32),
        ),
        in_specs=[pl.BlockSpec(memory_space=pltpu.VMEM)] * len(operands),
        out_specs=[pl.BlockSpec(memory_space=pltpu.VMEM)] * 4,
        scratch_shapes=[
            tile,
            tile,
            tile,
            tile,
            wide,
            wide,
            wide,
            tile,
            tile,
            tile,
            tile,
            pltpu.VMEM((HEADS_F, FINE, FINE), F32),
            pltpu.VMEM((3, FINE, FINE), BF16),
            pltpu.VMEM((8, PAD, 2 * channels), BF16),
            pltpu.VMEM((7, PAD, 2 * channels), BF16),
            pltpu.VMEM((PAD, 2 * channels), BF16),
            pltpu.VMEM((3, PAD, 2 * channels), BF16),
            pltpu.VMEM((8, PAD, 2 * channels), BF16),
            pltpu.SemaphoreType.DMA((35,)),
            pltpu.SemaphoreType.DMA((35,)),
        ],
        compiler_params=pltpu.CompilerParams(
            collective_id=0, has_side_effects=True, vmem_limit_bytes=48 * 2**20
        ),
    )(*operands)
    if not reduces:
        grad_qkv, grad_proj = lax.psum((grad_qkv, grad_proj), ("lon", "lat"))
    return (
        prediction.reshape(fields.shape),
        grad_input.reshape(fields.shape),
        grad_qkv,
        grad_proj,
    )

def solution(mesh):
    lat_size, lon_size = mesh.shape["lat"], mesh.shape["lon"]
    sizes = (lat_size, lon_size, lat_size == 2 and lon_size == 16)
    split = P(None, "lat", "lon", None)
    placed = (split, split, P("lat", "lon"), P("lat", "lon")) + (P(),) * 14
    return jax.shard_map(
        functools.partial(per_device, sizes),
        mesh=mesh,
        in_specs=placed,
        out_specs=(split, split, P(), P()),
        check_vma=False,
    )
```

```python
import functools
import math

import jax
import jax.numpy as jnp
import numpy as np
from jax import lax
from jax.experimental import pallas as pl
from jax.experimental.pallas import tpu as pltpu
from jax.sharding import PartitionSpec as P

HEADS_F = 6
WLAT = 6
WLON = 12
PAD = 48
FINE = 4 * PAD
TOKENS = 2 * WLAT * WLON
MESH = pl.DeviceIdType.MESH
F32 = jnp.float32
BF16 = jnp.bfloat16

epsilon = 1e-05
gelu_coeff = 0.7978845608028654


def layer_norm(values, gain_vec):
    average = jnp.mean(values, axis=-1, keepdims=True)
    centred = values - average
    spread = jnp.mean(centred * centred, axis=-1, keepdims=True)
    return centred * lax.rsqrt(spread + epsilon) * gain_vec


def layer_norm_back(values, gain_vec, upstream):
    average = jnp.mean(values, axis=-1, keepdims=True)
    centred = values - average
    spread = jnp.mean(centred * centred, axis=-1, keepdims=True)
    inverse = lax.rsqrt(spread + epsilon)
    normal = centred * inverse
    scaled = upstream * gain_vec
    return inverse * (
        scaled
        - jnp.mean(scaled, axis=-1, keepdims=True)
        - normal * jnp.mean(scaled * normal, axis=-1, keepdims=True)
    )


def gelu_tanh(values):
    inner = gelu_coeff * (values + 0.044715 * values * values * values)
    return 0.5 * values * (1.0 + jnp.tanh(inner))


def gelu_slope(values):
    inner = gelu_coeff * (values + 0.044715 * values * values * values)
    tangent = jnp.tanh(inner)
    return 0.5 * (1.0 + tangent) + 0.5 * values * (1.0 - tangent * tangent) * gelu_coeff * (
        1.0 + 3.0 * 0.044715 * values * values
    )


def iota(shape, axis):
    return lax.broadcasted_iota(jnp.int32, shape, axis)


def one_hot(rows, cols):
    return jnp.where(rows == cols, 1.0, 0.0).astype(BF16)


def natural_of(parity):
    group, place = parity // PAD, parity % PAD
    row = place // 6 % 3 * 2 + group // 2
    col = place % 6 * 2 + group % 2
    return jnp.where(place < 36, (row * WLON + col) * 2 + place // 18, -1)


def parity_of(quadrant):
    corner, place = quadrant // PAD, quadrant % PAD
    row = place // 6 % 3 + corner // 2 * 3
    col = place % 6 + corner % 2 * 6
    spot = (place // 18 * 3 + row // 2) * 6 + col // 2
    return jnp.where(place < 36, (row % 2 * 2 + col % 2) * PAD + spot, -1)


def dot(a, b):
    return jnp.dot(a, b, preferred_element_type=F32)

def dot_nt(a, b):
    return lax.dot_general(a, b, (((1,), (1,)), ((), ())), preferred_element_type=F32)

def blocks(tensor):
    return [tensor[g * PAD : (g + 1) * PAD] for g in range(4)]

def wide_mean(parts):
    total = parts[0]
    for part in parts[1:]:
        total = total + part
    return jnp.sum(total, axis=-1, keepdims=True) * (1.0 / (4 * total.shape[-1]))

def row_of(ref):
    return ref[...].reshape(1, -1)


def flip(index, bit):
    return index + bit * (1 - 2 * (index // bit % 2))

NAMES = (
    "orography",
    "land_sea",
    "both",
    "table",
    "land_vec",
    "gain_attn",
    "w_qkv",
    "w_up",
    "w_cproj",
    "w_proj",
    "gain_mlp",
    "w_in",
    "w_out",
    "gain_merge",
    "w_merge",
    "gain_coarse",
    "w_cqkv",
)


VMEM_BYTES = 61 * 2**20


def kernel(sizes, *refs):
    count = len(NAMES)
    sources = refs[:count]
    pred_out, gin_out, gqkv_out, gproj_out = refs[count : count + 4]
    local = refs[count + 4 : 2 * count + 4]
    (
        norm_send,
        norm_win,
        att_win,
        att_back,
        heads_send,
        heads_recv,
        back_send,
        back_recv,
        joined,
        gres_send,
        gres_win,
        groll_win,
        groll_back,
        probs_f,
        reduce_send,
        reduce_recv,
        line_send,
        line_recv,
        gathered,
        send_sem,
        recv_sem,
        load_sem,
    ) = refs[2 * count + 4 :]
    loads = {
        name: pltpu.make_async_copy(sources[n], local[n], load_sem.at[n])
        for n, name in enumerate(NAMES)
    }
    for name in NAMES:
        loads[name].start()

    def need(*names):
        refs_of = []
        for name in names:
            loads[name].wait()
            refs_of.append(local[NAMES.index(name)])
        return refs_of

    lat_size, lon_size, reduces = sizes
    i = lax.axis_index("lat")
    j = lax.axis_index("lon")

    def at(lat, lon):
        return (lax.rem(lon + lon_size, lon_size), lax.rem(lat + lat_size, lat_size))

    ahead = [at(i, j + 1), at(i + 1, j), at(i + 1, j + 1)]
    behind = [at(i, j - 1), at(i - 1, j), at(i - 1, j - 1)]
    group = [(flip(j, 1), i), (j, flip(i, 1)), (flip(j, 1), flip(i, 1))]
    greeted = ahead + behind + group
    plane, line = [], []
    if reduces:
        for d in range(1, 8):
            lat = flip(i, 1) if d & 4 else i
            lon = flip(j, 2) if d & 2 else j
            lon = flip(lon, 1) if d & 1 else lon
            plane.append((lon, lat))
        for d in range(1, 4):
            lon = flip(j, 8) if d & 2 else j
            lon = flip(lon, 4) if d & 1 else lon
            line.append((lon, i))
        greeted = greeted + plane + line
    barrier = pltpu.get_barrier_semaphore()
    for device in greeted:
        pl.semaphore_signal(barrier, inc=1, device_id=device, device_id_type=MESH)

    started = []

    def send(source, target, device):
        n = len(started)
        copy = pltpu.make_async_remote_copy(
            src_ref=source,
            dst_ref=target,
            send_sem=send_sem.at[n],
            recv_sem=recv_sem.at[n],
            device_id=device,
            device_id_type=MESH,
        )
        copy.start()
        started.append(copy)
        return copy

    def exchange(source, target, devices):
        return [send(source.at[s + 1], target.at[s + 1], devices[s]) for s in range(3)]

    def arrive(copies):
        for copy in copies:
            copy.wait_recv()

    def place(ref, tensor):
        for g, part in enumerate(blocks(tensor)):
            ref[g] = part

    def whole(ref):
        return jnp.concatenate([ref[g] for g in range(4)], axis=0)

    root = 1.0 / math.sqrt(32.0)

    def give(out, tensor):
        out[...] = dot(to_natural, tensor.astype(BF16)).astype(BF16)

    upright, along = iota((FINE, 1), 0), iota((1, FINE), 1)
    to_parity = one_hot(natural_of(upright), along[:, :TOKENS])
    to_natural = one_hot(upright[:TOKENS], natural_of(along))
    to_quadrant = one_hot(parity_of(upright), along)
    from_quadrant = one_hot(upright, parity_of(along))
    eye = one_hot(upright, along)
    orography, land_sea, both = need("orography", "land_sea", "both")
    pick_row = iota((TOKENS, WLAT), 0) // (2 * WLON) == iota((TOKENS, WLAT), 1)
    pick_row = jnp.where(pick_row, 1.0, 0.0).astype(BF16)
    pick_col = iota((TOKENS, WLON), 0) // 2 % WLON == iota((TOKENS, WLON), 1)

    def per_token(ref):
        rows = dot(pick_row, ref[...].astype(F32).astype(BF16))
        return jnp.sum(jnp.where(pick_col, rows, 0.0), axis=1, keepdims=True)

    table, land_vec, gain_attn = need("table", "land_vec", "gain_attn")
    kinds = table.shape[0]
    lanes = iota((TOKENS, 128), 1).astype(F32)
    land = jnp.where(lanes == kinds, per_token(land_sea), 0.0)
    classes = jnp.where(lanes == per_token(orography), 1.0, land).astype(BF16)
    classes = dot(to_parity, classes)
    surface = jnp.dot(classes[:, :kinds], table[...], precision=lax.Precision.HIGHEST)
    surface = classes[:, kinds : kinds + 1] * row_of(land_vec) + surface
    base = dot(to_parity, both[0]) + surface
    normed = layer_norm(base, row_of(gain_attn)).astype(BF16)
    place(norm_send, dot(to_quadrant, normed).astype(BF16))
    norm_win[0] = norm_send[0]
    pl.semaphore_wait(barrier, len(greeted))
    moves = exchange(norm_send, norm_win, ahead)

    w_up, w_cproj = need("w_up", "w_cproj")
    channels = w_up.shape[1] // 4
    coarse = w_cproj.shape[0]
    cot = dot(to_parity, both[1])
    cot_bf = blocks(cot.astype(BF16))
    grad_cnext = sum(
        dot_nt(cot_bf[g], w_up[:, g * channels : (g + 1) * channels]) for g in range(4)
    )
    grad_cout = dot_nt(grad_cnext.astype(BF16), w_cproj[...]).astype(BF16)
    share = coarse // 4

    def hand_out(column, tensor):
        for r in range(4):
            heads_send[r, :, column * share : (column + 1) * share] = tensor[
                :, r * share : (r + 1) * share
            ]

    hand_out(3, grad_cout)
    key_ids = iota((FINE, FINE), 0)
    query_ids = iota((FINE, FINE), 1)
    edge = jnp.where(i == 0, 1, 0)
    same = (key_ids // (2 * PAD) - query_ids // (2 * PAD)) * edge == 0
    real = key_ids % PAD < 36
    fine_bias = jnp.where(jnp.logical_and(same, real), 0.0, -1e30)
    coarse_bias = jnp.where(real, 0.0, -1e30)
    head_f = iota((FINE, channels), 1) // 32

    arrive(moves)
    rolled = whole(norm_win)
    (w_qkv,) = need("w_qkv")
    w_q = w_qkv[:, :channels]
    w_k = w_qkv[:, channels : 2 * channels]
    w_v = w_qkv[:, 2 * channels :]
    q = dot(rolled, w_q).astype(BF16)
    k = dot(rolled, w_k).astype(BF16)
    v = dot(rolled, w_v).astype(BF16)
    zero = jnp.zeros_like(q)
    v_turned = dot_nt(eye, v).astype(BF16)
    att_turned = []
    for h in range(HEADS_F):
        scores = dot_nt(jnp.where(head_f == h, k, zero), q) * root + fine_bias
        expon = jnp.exp(scores - jnp.max(scores, axis=0, keepdims=True))
        probs = expon * (1.0 / jnp.sum(expon, axis=0, keepdims=True))
        probs_f[h] = probs
        att_turned.append(dot(v_turned[32 * h : 32 * h + 32], probs.astype(BF16)))
    att = dot_nt(eye, jnp.concatenate(att_turned, axis=0).astype(BF16)).astype(BF16)

    place(att_win, att)
    att_back[0] = att_win[0]
    moves = exchange(att_win, att_back, behind)
    w_proj, gain_mlp, w_in, w_out, gain_merge, w_merge, gain_coarse, w_cqkv = need("w_proj", "gain_mlp", "w_in", "w_out", "gain_merge", "w_merge", "gain_coarse", "w_cqkv")
    arrive(moves)
    restored = dot(from_quadrant, whole(att_back)).astype(BF16)

    first = base + dot(restored, w_proj[...])
    mlp_in = layer_norm(first, row_of(gain_mlp)).astype(BF16)
    pre = dot(mlp_in, w_in[...])
    second = first + dot_nt(gelu_tanh(pre).astype(BF16), w_out[...])

    merged = blocks(second)
    gain_row = row_of(gain_merge)
    gains = [gain_row[:, g * channels : (g + 1) * channels] for g in range(4)]
    average = wide_mean(merged)
    centred = [part - average for part in merged]
    inverse = lax.rsqrt(wide_mean([part * part for part in centred]) + epsilon)
    normal = [part * inverse for part in centred]
    coarse_base = sum(
        dot((normal[g] * gains[g]).astype(BF16), w_merge[g * channels : (g + 1) * channels, :])
        for g in range(4)
    )
    coarse_norm = layer_norm(coarse_base, row_of(gain_coarse)).astype(BF16)
    coarse_qkv = dot(coarse_norm, w_cqkv[...]).astype(BF16)
    for column in range(3):
        hand_out(column, coarse_qkv[:, column * coarse : (column + 1) * coarse])
    rank = i % 2 * 2 + j % 2
    moves = [
        send(heads_send.at[lat % 2 * 2 + lon % 2], heads_recv.at[s + 1], (lon, lat))
        for s, (lon, lat) in enumerate(group)
    ]
    heads_recv[0] = heads_send[rank]
    arrive(moves)

    gathered_in = whole(heads_recv)
    cq, ck, cv, cdo = (gathered_in[:, n * share : (n + 1) * share] for n in range(4))
    head_c = iota((FINE, share), 1) // 32
    none = jnp.zeros_like(cq)
    cv_turned = dot_nt(eye[:share, :share], cv).astype(BF16)
    ck_turned = dot_nt(eye[:share, :share], ck).astype(BF16)
    grad_cv = jnp.zeros((FINE, share), F32)
    grad_ck = jnp.zeros((FINE, share), F32)
    turned = []
    for h in range(share // 32):
        mine = head_c == h
        scores = dot_nt(jnp.where(mine, ck, none), cq) * root + coarse_bias
        expon = jnp.exp(scores - jnp.max(scores, axis=0, keepdims=True))
        probs = expon * (1.0 / jnp.sum(expon, axis=0, keepdims=True))
        soft = probs.astype(BF16)
        soft_grad = dot_nt(jnp.where(mine, cv, none), cdo)
        kept = jnp.sum(soft_grad * probs, axis=0, keepdims=True)
        score_grad = (probs * (soft_grad - kept)).astype(BF16)
        grad_cv = grad_cv + dot(soft, jnp.where(mine, cdo, none))
        grad_ck = grad_ck + dot(score_grad, jnp.where(mine, cq, none))
        rows = slice(32 * h, 32 * h + 32)
        turned.append((dot(ck_turned[rows], score_grad) * root, dot(cv_turned[rows], soft)))
    grad_cq, coarse_out = (
        dot_nt(eye, jnp.concatenate(part, axis=0).astype(BF16)) for part in zip(*turned)
    )
    results = (grad_cq, grad_ck * root, grad_cv, coarse_out)
    for n, part in enumerate(results):
        for s in range(4):
            rows = slice(s * PAD, (s + 1) * PAD)
            back_send[s, :, n * share : (n + 1) * share] = part[rows].astype(BF16)
    moves = [
        send(back_send.at[s + 1], back_recv.at[rank], device) for s, device in enumerate(group)
    ]
    back_recv[rank] = back_send[0]
    arrive(moves)

    for n in range(4):
        for r in range(4):
            start = n * coarse + r * share
            joined[:, start : start + share] = back_recv[r, :, n * share : (n + 1) * share]
    grad_cnorm = dot_nt(joined[:, : 3 * coarse], w_cqkv[...])
    grad_cbase = grad_cnext + layer_norm_back(coarse_base, row_of(gain_coarse), grad_cnorm)
    grad_cbase = grad_cbase.astype(BF16)
    scaled = [
        dot_nt(grad_cbase, w_merge[g * channels : (g + 1) * channels, :]) * gains[g]
        for g in range(4)
    ]
    mean_scaled = wide_mean(scaled)
    mean_both = wide_mean([scaled[g] * normal[g] for g in range(4)])
    grad_merged = [
        inverse * (scaled[g] - mean_scaled - normal[g] * mean_both) for g in range(4)
    ]
    grad_second = cot + jnp.concatenate(grad_merged, axis=0)
    grad_active = dot(grad_second.astype(BF16), w_out[...])
    grad_pre = (grad_active * gelu_slope(pre)).astype(BF16)
    grad_mlp_in = dot_nt(grad_pre, w_in[...])
    grad_first = grad_second + layer_norm_back(first, row_of(gain_mlp), grad_mlp_in)
    grad_first_bf = grad_first.astype(BF16)
    grad_restored = dot_nt(grad_first_bf, w_proj[...]).astype(BF16)
    place(gres_send, dot(to_quadrant, grad_restored).astype(BF16))
    gres_win[0] = gres_send[0]
    moves = exchange(gres_send, gres_win, ahead)
    grad_proj = dot(dot_nt(eye, restored).astype(BF16), grad_first_bf)
    coarse_next = (coarse_base + dot(joined[:, 3 * coarse :], w_cproj[...])).astype(BF16)
    upward = jnp.concatenate(
        [dot(coarse_next, w_up[:, g * channels : (g + 1) * channels]) for g in range(4)], axis=0
    )
    give(pred_out, second + upward)
    k_turned = dot_nt(eye, k).astype(BF16)
    rolled_turned = dot_nt(eye, rolled).astype(BF16)
    arrive(moves)

    do = whole(gres_win)
    grad_v = jnp.zeros((FINE, channels), F32)
    grad_k = jnp.zeros((FINE, channels), F32)
    gq_turned = []
    for h in range(HEADS_F):
        mine = head_f == h
        probs = probs_f[h]
        soft_grad = dot_nt(jnp.where(mine, v, zero), do)
        kept = jnp.sum(soft_grad * probs, axis=0, keepdims=True)
        score_grad = (probs * (soft_grad - kept)).astype(BF16)
        grad_v = grad_v + dot(probs.astype(BF16), jnp.where(mine, do, zero))
        grad_k = grad_k + dot(score_grad, jnp.where(mine, q, zero))
        gq_turned.append(dot(k_turned[32 * h : 32 * h + 32], score_grad) * root)
    grad_q = dot_nt(eye, jnp.concatenate(gq_turned, axis=0).astype(BF16)).astype(BF16)
    grad_k = (grad_k * root).astype(BF16)
    grad_v = grad_v.astype(BF16)
    grad_rolled = dot_nt(grad_q, w_q) + dot_nt(grad_k, w_k) + dot_nt(grad_v, w_v)
    place(groll_win, grad_rolled.astype(BF16))
    groll_back[0] = groll_win[0]
    moves = exchange(groll_win, groll_back, behind)

    part_q = dot(rolled_turned, grad_q)
    part_k = dot(rolled_turned, grad_k)
    part_v = dot(rolled_turned, grad_v)
    if reduces:
        for g in range(4):
            rows = slice(g * PAD, (g + 1) * PAD)
            reduce_send[g, :, :channels] = part_q[rows].astype(BF16)
            reduce_send[g, :, channels:] = part_k[rows].astype(BF16)
            reduce_send[4 + g, :, :channels] = part_v[rows].astype(BF16)
            reduce_send[4 + g, :, channels:] = grad_proj[rows].astype(BF16)
        me = i * 4 + j % 4
        to_owner = [
            send(reduce_send.at[lat * 4 + lon % 4], reduce_recv.at[d], (lon, lat))
            for d, (lon, lat) in enumerate(plane)
        ]
    else:
        gqkv_out[:, :channels] = part_q
        gqkv_out[:, channels : 2 * channels] = part_k
        gqkv_out[:, 2 * channels :] = part_v
        gproj_out[...] = grad_proj

    arrive(moves)
    grad_normed = dot(from_quadrant, whole(groll_back))
    grad_base = grad_first + layer_norm_back(base, row_of(gain_attn), grad_normed)
    give(gin_out, grad_base)

    if reduces:
        arrive(to_owner)
        total = reduce_send[me].astype(F32)
        for d in range(7):
            total = total + reduce_recv[d].astype(F32)
        line_send[...] = total.astype(BF16)
        moves = [send(line_send, line_recv.at[d], line[d]) for d in range(3)]
        arrive(moves)
        total = (line_send[...].astype(F32) + line_recv[0].astype(F32)) + (
            line_recv[1].astype(F32) + line_recv[2].astype(F32)
        )
        gathered[me] = total.astype(BF16)
        moves = [send(gathered.at[me], gathered.at[me], device) for device in plane]
        arrive(moves)
        for g in range(4):
            rows = slice(g * PAD, (g + 1) * PAD)
            left = gathered[g].astype(F32)
            right = gathered[4 + g].astype(F32)
            gqkv_out[rows, : 2 * channels] = left
            gqkv_out[rows, 2 * channels :] = right[:, :channels]
            gproj_out[rows, :] = right[:, channels:]
    for copy in started:
        copy.wait_send()

def per_device(
    sizes,
    fields,
    cotangent,
    land_sea,
    orography,
    land_vec,
    orog_table,
    gain_attn,
    w_qkv,
    w_proj,
    gain_mlp,
    w_in,
    w_out,
    gain_merge,
    w_merge,
    gain_coarse,
    w_cqkv,
    w_cproj,
    w_up,
):
    reduces = sizes[2]
    channels = fields.shape[-1]
    coarse = w_cproj.shape[0]
    def flat(tensor):
        return tensor.transpose(1, 2, 0, 3).reshape(TOKENS, channels)

    both = jnp.stack([flat(fields), flat(cotangent)])
    known = dict(
        orography=orography,
        land_sea=land_sea,
        both=both,
        table=orog_table,
        land_vec=land_vec,
        gain_attn=gain_attn,
        w_qkv=w_qkv,
        w_up=w_up,
        w_cproj=w_cproj,
        w_proj=w_proj,
        gain_mlp=gain_mlp,
        w_in=w_in,
        w_out=w_out.T,
        gain_merge=gain_merge,
        w_merge=w_merge,
        gain_coarse=gain_coarse,
        w_cqkv=w_cqkv,
    )
    operands = [known[name] for name in NAMES]
    tile = pltpu.VMEM((4, PAD, channels), BF16)
    wide = pltpu.VMEM((4, PAD, coarse), BF16)
    prediction, grad_input, grad_qkv, grad_proj = pl.pallas_call(
        functools.partial(kernel, sizes),
        out_shape=(
            jax.ShapeDtypeStruct((TOKENS, channels), BF16),
            jax.ShapeDtypeStruct((TOKENS, channels), BF16),
            jax.ShapeDtypeStruct((channels, 3 * channels), F32),
            jax.ShapeDtypeStruct((channels, channels), F32),
        ),
        in_specs=[pl.BlockSpec(memory_space=pltpu.HBM)] * len(operands),
        out_specs=[pl.BlockSpec(memory_space=pltpu.VMEM)] * 4,
        scratch_shapes=[pltpu.VMEM(x.shape, x.dtype) for x in operands]
        + [
            tile,
            tile,
            tile,
            tile,
            wide,
            wide,
            wide,
            wide,
            pltpu.VMEM((PAD, 4 * coarse), BF16),
            tile,
            tile,
            tile,
            tile,
            pltpu.VMEM((HEADS_F, FINE, FINE), F32),
            pltpu.VMEM((8, PAD, 2 * channels), BF16),
            pltpu.VMEM((7, PAD, 2 * channels), BF16),
            pltpu.VMEM((PAD, 2 * channels), BF16),
            pltpu.VMEM((3, PAD, 2 * channels), BF16),
            pltpu.VMEM((8, PAD, 2 * channels), BF16),
            pltpu.SemaphoreType.DMA((35,)),
            pltpu.SemaphoreType.DMA((35,)),
            pltpu.SemaphoreType.DMA((len(operands),)),
        ],
        compiler_params=pltpu.CompilerParams(
            collective_id=0, has_side_effects=True, vmem_limit_bytes=VMEM_BYTES
        ),
    )(*operands)
    if not reduces:
        grad_qkv, grad_proj = lax.psum((grad_qkv, grad_proj), ("lon", "lat"))

    def unflat(tensor):
        return tensor.reshape(WLAT, WLON, 2, channels).transpose(2, 0, 1, 3)

    return (
        unflat(prediction),
        unflat(grad_input),
        grad_qkv,
        grad_proj,
    )

def solution(mesh):
    lat_size, lon_size = mesh.shape["lat"], mesh.shape["lon"]
    sizes = (lat_size, lon_size, lat_size == 2 and lon_size == 16)
    split = P(None, "lat", "lon", None)
    placed = (split, split, P("lat", "lon"), P("lat", "lon")) + (P(),) * 14
    return jax.shard_map(
        functools.partial(per_device, sizes),
        mesh=mesh,
        in_specs=placed,
        out_specs=(split, split, P(), P()),
        check_vma=False,
    )
```

```python
import functools
import math

import jax
import jax.numpy as jnp
import numpy as np
from jax import lax
from jax.experimental import pallas as pl
from jax.experimental.pallas import tpu as pltpu
from jax.sharding import PartitionSpec as P

HEADS_F = 6
WLAT = 6
WLON = 12
PAD = 48
FINE = 4 * PAD
TOKENS = 2 * WLAT * WLON
MESH = pl.DeviceIdType.MESH
F32 = jnp.float32
BF16 = jnp.bfloat16

epsilon = 1e-05
gelu_coeff = 0.7978845608028654


def layer_norm(values, gain_vec):
    average = jnp.mean(values, axis=-1, keepdims=True)
    centred = values - average
    spread = jnp.mean(centred * centred, axis=-1, keepdims=True)
    return centred * lax.rsqrt(spread + epsilon) * gain_vec


def layer_norm_back(values, gain_vec, upstream):
    average = jnp.mean(values, axis=-1, keepdims=True)
    centred = values - average
    spread = jnp.mean(centred * centred, axis=-1, keepdims=True)
    inverse = lax.rsqrt(spread + epsilon)
    normal = centred * inverse
    scaled = upstream * gain_vec
    return inverse * (
        scaled
        - jnp.mean(scaled, axis=-1, keepdims=True)
        - normal * jnp.mean(scaled * normal, axis=-1, keepdims=True)
    )


def gelu_tanh(values):
    inner = gelu_coeff * (values + 0.044715 * values * values * values)
    return 0.5 * values * (1.0 + jnp.tanh(inner))


def gelu_slope(values):
    inner = gelu_coeff * (values + 0.044715 * values * values * values)
    tangent = jnp.tanh(inner)
    return 0.5 * (1.0 + tangent) + 0.5 * values * (1.0 - tangent * tangent) * gelu_coeff * (
        1.0 + 3.0 * 0.044715 * values * values
    )


def iota(shape, axis):
    return lax.broadcasted_iota(jnp.int32, shape, axis)


def one_hot(rows, cols):
    return jnp.where(rows == cols, 1.0, 0.0).astype(BF16)


def natural_of(parity):
    group, place = parity // PAD, parity % PAD
    row = place // 6 % 3 * 2 + group // 2
    col = place % 6 * 2 + group % 2
    return jnp.where(place < 36, (row * WLON + col) * 2 + place // 18, -1)


def parity_of(quadrant):
    corner, place = quadrant // PAD, quadrant % PAD
    row = place // 6 % 3 + corner // 2 * 3
    col = place % 6 + corner % 2 * 6
    spot = (place // 18 * 3 + row // 2) * 6 + col // 2
    return jnp.where(place < 36, (row % 2 * 2 + col % 2) * PAD + spot, -1)


def dot(a, b):
    return jnp.dot(a, b, preferred_element_type=F32)

def dot_nt(a, b):
    return lax.dot_general(a, b, (((1,), (1,)), ((), ())), preferred_element_type=F32)

def blocks(tensor):
    return [tensor[g * PAD : (g + 1) * PAD] for g in range(4)]

def wide_mean(parts):
    total = parts[0]
    for part in parts[1:]:
        total = total + part
    return jnp.sum(total, axis=-1, keepdims=True) * (1.0 / (4 * total.shape[-1]))

def row_of(ref):
    return ref[...].reshape(1, -1)


def flip(index, bit):
    return index + bit * (1 - 2 * (index // bit % 2))

NAMES = (
    "orography",
    "land_sea",
    "both",
    "table",
    "land_vec",
    "gain_attn",
    "w_qkv",
    "w_up",
    "w_cproj",
    "w_proj",
    "gain_mlp",
    "w_in",
    "w_out",
    "gain_merge",
    "w_merge",
    "gain_coarse",
    "w_cqkv",
)


VMEM_BYTES = 61 * 2**20


def kernel(sizes, *refs):
    count = len(NAMES)
    sources = refs[:count]
    pred_out, gin_out, gqkv_out, gproj_out = refs[count : count + 4]
    local = refs[count + 4 : 2 * count + 4]
    (
        norm_send,
        norm_win,
        att_win,
        att_back,
        heads_send,
        heads_recv,
        back_send,
        back_recv,
        joined,
        gres_send,
        gres_win,
        groll_win,
        groll_back,
        probs_f,
        reduce_send,
        reduce_recv,
        line_send,
        line_recv,
        gathered,
        send_sem,
        recv_sem,
        load_sem,
    ) = refs[2 * count + 4 :]
    loads = {
        name: pltpu.make_async_copy(sources[n], local[n], load_sem.at[n])
        for n, name in enumerate(NAMES)
    }
    for name in NAMES:
        loads[name].start()

    def need(*names):
        refs_of = []
        for name in names:
            loads[name].wait()
            refs_of.append(local[NAMES.index(name)])
        return refs_of

    lat_size, lon_size, reduces = sizes
    i = lax.axis_index("lat")
    j = lax.axis_index("lon")

    def at(lat, lon):
        return (lax.rem(lon + lon_size, lon_size), lax.rem(lat + lat_size, lat_size))

    ahead = [at(i, j + 1), at(i + 1, j), at(i + 1, j + 1)]
    behind = [at(i, j - 1), at(i - 1, j), at(i - 1, j - 1)]
    group = [(flip(j, 1), i), (j, flip(i, 1)), (flip(j, 1), flip(i, 1))]
    greeted = ahead + behind + group
    plane, line = [], []
    if reduces:
        for d in range(1, 8):
            lat = flip(i, 1) if d & 4 else i
            lon = flip(j, 2) if d & 2 else j
            lon = flip(lon, 1) if d & 1 else lon
            plane.append((lon, lat))
        for d in range(1, 4):
            lon = flip(j, 8) if d & 2 else j
            lon = flip(lon, 4) if d & 1 else lon
            line.append((lon, i))
        greeted = greeted + plane + line
    barrier = pltpu.get_barrier_semaphore()
    for device in greeted:
        pl.semaphore_signal(barrier, inc=1, device_id=device, device_id_type=MESH)

    started = []

    def send(source, target, device):
        n = len(started)
        copy = pltpu.make_async_remote_copy(
            src_ref=source,
            dst_ref=target,
            send_sem=send_sem.at[n],
            recv_sem=recv_sem.at[n],
            device_id=device,
            device_id_type=MESH,
        )
        copy.start()
        started.append(copy)
        return copy

    def exchange(source, target, devices):
        return [send(source.at[s + 1], target.at[s + 1], devices[s]) for s in range(3)]

    def arrive(copies):
        for copy in copies:
            copy.wait_recv()

    def place(ref, tensor):
        for g, part in enumerate(blocks(tensor)):
            ref[g] = part

    def whole(ref):
        return jnp.concatenate([ref[g] for g in range(4)], axis=0)

    root = 1.0 / math.sqrt(32.0)

    def give(out, tensor):
        out[...] = dot(to_natural, tensor.astype(BF16)).astype(BF16)

    upright, along = iota((FINE, 1), 0), iota((1, FINE), 1)
    to_parity = one_hot(natural_of(upright), along[:, :TOKENS])
    to_natural = one_hot(upright[:TOKENS], natural_of(along))
    to_quadrant = one_hot(parity_of(upright), along)
    from_quadrant = one_hot(upright, parity_of(along))
    eye = one_hot(upright, along)
    orography, land_sea, both = need("orography", "land_sea", "both")
    pick_row = iota((TOKENS, WLAT), 0) // (2 * WLON) == iota((TOKENS, WLAT), 1)
    pick_row = jnp.where(pick_row, 1.0, 0.0).astype(BF16)
    pick_col = iota((TOKENS, WLON), 0) // 2 % WLON == iota((TOKENS, WLON), 1)

    def per_token(ref):
        rows = dot(pick_row, ref[...].astype(F32).astype(BF16))
        return jnp.sum(jnp.where(pick_col, rows, 0.0), axis=1, keepdims=True)

    table, land_vec, gain_attn = need("table", "land_vec", "gain_attn")
    kinds = table.shape[0]
    lanes = iota((TOKENS, 128), 1).astype(F32)
    land = jnp.where(lanes == kinds, per_token(land_sea), 0.0)
    classes = jnp.where(lanes == per_token(orography), 1.0, land).astype(BF16)
    classes = dot(to_parity, classes)
    surface = jnp.dot(classes[:, :kinds], table[...], precision=lax.Precision.HIGHEST)
    surface = classes[:, kinds : kinds + 1] * row_of(land_vec) + surface
    base = dot(to_parity, both[0]) + surface
    normed = layer_norm(base, row_of(gain_attn)).astype(BF16)
    place(norm_send, dot(to_quadrant, normed).astype(BF16))
    norm_win[0] = norm_send[0]
    pl.semaphore_wait(barrier, len(greeted))
    moves = exchange(norm_send, norm_win, ahead)

    w_up, w_cproj = need("w_up", "w_cproj")
    channels = w_up.shape[1] // 4
    coarse = w_cproj.shape[0]
    cot = dot(to_parity, both[1])
    cot_bf = blocks(cot.astype(BF16))
    grad_cnext = sum(
        dot_nt(cot_bf[g], w_up[:, g * channels : (g + 1) * channels]) for g in range(4)
    )
    grad_cout = dot_nt(grad_cnext.astype(BF16), w_cproj[...]).astype(BF16)
    share = coarse // 4

    def hand_out(column, tensor):
        for r in range(4):
            heads_send[r, :, column * share : (column + 1) * share] = tensor[
                :, r * share : (r + 1) * share
            ]

    hand_out(3, grad_cout)
    key_ids = iota((FINE, FINE), 0)
    query_ids = iota((FINE, FINE), 1)
    edge = jnp.where(i == 0, 1, 0)
    same = (key_ids // (2 * PAD) - query_ids // (2 * PAD)) * edge == 0
    real = key_ids % PAD < 36
    fine_bias = jnp.where(jnp.logical_and(same, real), 0.0, -1e30)
    coarse_bias = jnp.where(real, 0.0, -1e30)
    head_f = iota((FINE, channels), 1) // 32

    arrive(moves)
    rolled = whole(norm_win)
    (w_qkv,) = need("w_qkv")
    w_q = w_qkv[:, :channels]
    w_k = w_qkv[:, channels : 2 * channels]
    w_v = w_qkv[:, 2 * channels :]
    q = dot(rolled, w_q).astype(BF16)
    k = dot(rolled, w_k).astype(BF16)
    v = dot(rolled, w_v).astype(BF16)
    zero = jnp.zeros_like(q)
    v_turned = dot_nt(eye, v).astype(BF16)
    att_turned = []
    for h in range(HEADS_F):
        scores = dot_nt(jnp.where(head_f == h, k, zero), q) * root + fine_bias
        expon = jnp.exp(scores - jnp.max(scores, axis=0, keepdims=True))
        probs = expon * (1.0 / jnp.sum(expon, axis=0, keepdims=True))
        probs_f[h] = probs
        att_turned.append(dot(v_turned[32 * h : 32 * h + 32], probs.astype(BF16)))
    att = dot_nt(eye, jnp.concatenate(att_turned, axis=0).astype(BF16)).astype(BF16)

    place(att_win, att)
    att_back[0] = att_win[0]
    moves = exchange(att_win, att_back, behind)
    w_proj, gain_mlp, w_in, w_out, gain_merge, w_merge, gain_coarse, w_cqkv = need("w_proj", "gain_mlp", "w_in", "w_out", "gain_merge", "w_merge", "gain_coarse", "w_cqkv")
    arrive(moves)
    restored = dot(from_quadrant, whole(att_back)).astype(BF16)

    first = base + dot(restored, w_proj[...])
    mlp_in = layer_norm(first, row_of(gain_mlp)).astype(BF16)
    pre = dot(mlp_in, w_in[...])
    second = first + dot_nt(gelu_tanh(pre).astype(BF16), w_out[...])

    merged = blocks(second)
    gain_row = row_of(gain_merge)
    gains = [gain_row[:, g * channels : (g + 1) * channels] for g in range(4)]
    average = wide_mean(merged)
    centred = [part - average for part in merged]
    inverse = lax.rsqrt(wide_mean([part * part for part in centred]) + epsilon)
    normal = [part * inverse for part in centred]
    coarse_base = sum(
        dot((normal[g] * gains[g]).astype(BF16), w_merge[g * channels : (g + 1) * channels, :])
        for g in range(4)
    )
    coarse_norm = layer_norm(coarse_base, row_of(gain_coarse)).astype(BF16)
    coarse_qkv = dot(coarse_norm, w_cqkv[...]).astype(BF16)
    for column in range(3):
        hand_out(column, coarse_qkv[:, column * coarse : (column + 1) * coarse])
    rank = i % 2 * 2 + j % 2
    moves = [
        send(heads_send.at[lat % 2 * 2 + lon % 2], heads_recv.at[s + 1], (lon, lat))
        for s, (lon, lat) in enumerate(group)
    ]
    heads_recv[0] = heads_send[rank]
    arrive(moves)

    gathered_in = whole(heads_recv)
    cq, ck, cv, cdo = (gathered_in[:, n * share : (n + 1) * share] for n in range(4))
    head_c = iota((FINE, share), 1) // 32
    none = jnp.zeros_like(cq)
    cv_turned = dot_nt(eye[:share, :share], cv).astype(BF16)
    ck_turned = dot_nt(eye[:share, :share], ck).astype(BF16)
    grad_cv = jnp.zeros((FINE, share), F32)
    grad_ck = jnp.zeros((FINE, share), F32)
    turned = []
    for h in range(share // 32):
        mine = head_c == h
        scores = dot_nt(jnp.where(mine, ck, none), cq) * root + coarse_bias
        expon = jnp.exp(scores - jnp.max(scores, axis=0, keepdims=True))
        probs = expon * (1.0 / jnp.sum(expon, axis=0, keepdims=True))
        soft = probs.astype(BF16)
        soft_grad = dot_nt(jnp.where(mine, cv, none), cdo)
        kept = jnp.sum(soft_grad * probs, axis=0, keepdims=True)
        score_grad = (probs * (soft_grad - kept)).astype(BF16)
        grad_cv = grad_cv + dot(soft, jnp.where(mine, cdo, none))
        grad_ck = grad_ck + dot(score_grad, jnp.where(mine, cq, none))
        rows = slice(32 * h, 32 * h + 32)
        turned.append((dot(ck_turned[rows], score_grad) * root, dot(cv_turned[rows], soft)))
    grad_cq, coarse_out = (
        dot_nt(eye, jnp.concatenate(part, axis=0).astype(BF16)) for part in zip(*turned)
    )
    results = (grad_cq, grad_ck * root, grad_cv, coarse_out)
    for n, part in enumerate(results):
        for s in range(4):
            rows = slice(s * PAD, (s + 1) * PAD)
            back_send[s, :, n * share : (n + 1) * share] = part[rows].astype(BF16)
    moves = [
        send(back_send.at[s + 1], back_recv.at[rank], device) for s, device in enumerate(group)
    ]
    back_recv[rank] = back_send[0]
    arrive(moves)

    for n in range(4):
        for r in range(4):
            start = n * coarse + r * share
            joined[:, start : start + share] = back_recv[r, :, n * share : (n + 1) * share]
    grad_cnorm = dot_nt(joined[:, : 3 * coarse], w_cqkv[...])
    grad_cbase = grad_cnext + layer_norm_back(coarse_base, row_of(gain_coarse), grad_cnorm)
    grad_cbase = grad_cbase.astype(BF16)
    scaled = [
        dot_nt(grad_cbase, w_merge[g * channels : (g + 1) * channels, :]) * gains[g]
        for g in range(4)
    ]
    mean_scaled = wide_mean(scaled)
    mean_both = wide_mean([scaled[g] * normal[g] for g in range(4)])
    grad_merged = [
        inverse * (scaled[g] - mean_scaled - normal[g] * mean_both) for g in range(4)
    ]
    grad_second = cot + jnp.concatenate(grad_merged, axis=0)
    grad_active = dot(grad_second.astype(BF16), w_out[...])
    grad_pre = (grad_active * gelu_slope(pre)).astype(BF16)
    grad_mlp_in = dot_nt(grad_pre, w_in[...])
    grad_first = grad_second + layer_norm_back(first, row_of(gain_mlp), grad_mlp_in)
    grad_first_bf = grad_first.astype(BF16)
    grad_restored = dot_nt(grad_first_bf, w_proj[...]).astype(BF16)
    place(gres_send, dot(to_quadrant, grad_restored).astype(BF16))
    gres_win[0] = gres_send[0]
    moves = exchange(gres_send, gres_win, ahead)
    grad_proj = dot(dot_nt(eye, restored).astype(BF16), grad_first_bf)
    coarse_next = (coarse_base + dot(joined[:, 3 * coarse :], w_cproj[...])).astype(BF16)
    upward = jnp.concatenate(
        [dot(coarse_next, w_up[:, g * channels : (g + 1) * channels]) for g in range(4)], axis=0
    )
    give(pred_out, second + upward)
    k_turned = dot_nt(eye, k).astype(BF16)
    rolled_turned = dot_nt(eye, rolled).astype(BF16)
    arrive(moves)

    do = whole(gres_win)
    grad_v = jnp.zeros((FINE, channels), F32)
    grad_k = jnp.zeros((FINE, channels), F32)
    gq_turned = []
    for h in range(HEADS_F):
        mine = head_f == h
        probs = probs_f[h]
        soft_grad = dot_nt(jnp.where(mine, v, zero), do)
        kept = jnp.sum(soft_grad * probs, axis=0, keepdims=True)
        score_grad = (probs * (soft_grad - kept)).astype(BF16)
        grad_v = grad_v + dot(probs.astype(BF16), jnp.where(mine, do, zero))
        grad_k = grad_k + dot(score_grad, jnp.where(mine, q, zero))
        gq_turned.append(dot(k_turned[32 * h : 32 * h + 32], score_grad) * root)
    grad_q = dot_nt(eye, jnp.concatenate(gq_turned, axis=0).astype(BF16)).astype(BF16)
    grad_k = (grad_k * root).astype(BF16)
    grad_v = grad_v.astype(BF16)
    grad_rolled = dot_nt(grad_q, w_q) + dot_nt(grad_k, w_k) + dot_nt(grad_v, w_v)
    place(groll_win, grad_rolled.astype(BF16))
    groll_back[0] = groll_win[0]
    moves = exchange(groll_win, groll_back, behind)

    part_q = dot(rolled_turned, grad_q)
    part_k = dot(rolled_turned, grad_k)
    part_v = dot(rolled_turned, grad_v)
    if reduces:
        for g in range(4):
            rows = slice(g * PAD, (g + 1) * PAD)
            reduce_send[g, :, :channels] = part_q[rows].astype(BF16)
            reduce_send[g, :, channels:] = part_k[rows].astype(BF16)
            reduce_send[4 + g, :, :channels] = part_v[rows].astype(BF16)
            reduce_send[4 + g, :, channels:] = grad_proj[rows].astype(BF16)
        me = i * 4 + j % 4
        to_owner = [
            send(reduce_send.at[lat * 4 + lon % 4], reduce_recv.at[d], (lon, lat))
            for d, (lon, lat) in enumerate(plane)
        ]
    else:
        gqkv_out[:, :channels] = part_q
        gqkv_out[:, channels : 2 * channels] = part_k
        gqkv_out[:, 2 * channels :] = part_v
        gproj_out[...] = grad_proj

    arrive(moves)
    grad_normed = dot(from_quadrant, whole(groll_back))
    grad_base = grad_first + layer_norm_back(base, row_of(gain_attn), grad_normed)
    give(gin_out, grad_base)

    if reduces:
        arrive(to_owner)
        total = reduce_send[me].astype(F32)
        for d in range(7):
            total = total + reduce_recv[d].astype(F32)
        line_send[...] = total.astype(BF16)
        moves = [send(line_send, line_recv.at[d], line[d]) for d in range(3)]
        arrive(moves)
        total = (line_send[...].astype(F32) + line_recv[0].astype(F32)) + (
            line_recv[1].astype(F32) + line_recv[2].astype(F32)
        )
        gathered[me] = total.astype(BF16)
        moves = [send(gathered.at[me], gathered.at[me], device) for device in plane]
        arrive(moves)
        for g in range(4):
            rows = slice(g * PAD, (g + 1) * PAD)
            left = gathered[g]
            right = gathered[4 + g]
            gqkv_out[rows, : 2 * channels] = left
            gqkv_out[rows, 2 * channels :] = right[:, :channels]
            gproj_out[rows, :] = right[:, channels:]
    for copy in started:
        copy.wait_send()

def per_device(
    sizes,
    fields,
    cotangent,
    land_sea,
    orography,
    land_vec,
    orog_table,
    gain_attn,
    w_qkv,
    w_proj,
    gain_mlp,
    w_in,
    w_out,
    gain_merge,
    w_merge,
    gain_coarse,
    w_cqkv,
    w_cproj,
    w_up,
):
    reduces = sizes[2]
    channels = fields.shape[-1]
    coarse = w_cproj.shape[0]
    def flat(tensor):
        return tensor.transpose(1, 2, 0, 3).reshape(TOKENS, channels)

    both = jnp.stack([flat(fields), flat(cotangent)])
    known = dict(
        orography=orography,
        land_sea=land_sea,
        both=both,
        table=orog_table,
        land_vec=land_vec,
        gain_attn=gain_attn,
        w_qkv=w_qkv,
        w_up=w_up,
        w_cproj=w_cproj,
        w_proj=w_proj,
        gain_mlp=gain_mlp,
        w_in=w_in,
        w_out=w_out.T,
        gain_merge=gain_merge,
        w_merge=w_merge,
        gain_coarse=gain_coarse,
        w_cqkv=w_cqkv,
    )
    operands = [known[name] for name in NAMES]
    sum_type = BF16 if reduces else F32
    tile = pltpu.VMEM((4, PAD, channels), BF16)
    wide = pltpu.VMEM((4, PAD, coarse), BF16)
    prediction, grad_input, grad_qkv, grad_proj = pl.pallas_call(
        functools.partial(kernel, sizes),
        out_shape=(
            jax.ShapeDtypeStruct((TOKENS, channels), BF16),
            jax.ShapeDtypeStruct((TOKENS, channels), BF16),
            jax.ShapeDtypeStruct((channels, 3 * channels), sum_type),
            jax.ShapeDtypeStruct((channels, channels), sum_type),
        ),
        in_specs=[pl.BlockSpec(memory_space=pltpu.HBM)] * len(operands),
        out_specs=[pl.BlockSpec(memory_space=pltpu.VMEM)] * 4,
        scratch_shapes=[pltpu.VMEM(x.shape, x.dtype) for x in operands]
        + [
            tile,
            tile,
            tile,
            tile,
            wide,
            wide,
            wide,
            wide,
            pltpu.VMEM((PAD, 4 * coarse), BF16),
            tile,
            tile,
            tile,
            tile,
            pltpu.VMEM((HEADS_F, FINE, FINE), F32),
            pltpu.VMEM((8, PAD, 2 * channels), BF16),
            pltpu.VMEM((7, PAD, 2 * channels), BF16),
            pltpu.VMEM((PAD, 2 * channels), BF16),
            pltpu.VMEM((3, PAD, 2 * channels), BF16),
            pltpu.VMEM((8, PAD, 2 * channels), BF16),
            pltpu.SemaphoreType.DMA((35,)),
            pltpu.SemaphoreType.DMA((35,)),
            pltpu.SemaphoreType.DMA((len(operands),)),
        ],
        compiler_params=pltpu.CompilerParams(
            collective_id=0, has_side_effects=True, vmem_limit_bytes=VMEM_BYTES
        ),
    )(*operands)
    if not reduces:
        grad_qkv, grad_proj = lax.psum((grad_qkv, grad_proj), ("lon", "lat"))

    def unflat(tensor):
        return tensor.reshape(WLAT, WLON, 2, channels).transpose(2, 0, 1, 3)

    return (
        unflat(prediction),
        unflat(grad_input),
        grad_qkv.astype(F32),
        grad_proj.astype(F32),
    )

def solution(mesh):
    lat_size, lon_size = mesh.shape["lat"], mesh.shape["lon"]
    sizes = (lat_size, lon_size, lat_size == 2 and lon_size == 16)
    split = P(None, "lat", "lon", None)
    placed = (split, split, P("lat", "lon"), P("lat", "lon")) + (P(),) * 14
    return jax.shard_map(
        functools.partial(per_device, sizes),
        mesh=mesh,
        in_specs=placed,
        out_specs=(split, split, P(), P()),
        check_vma=False,
    )
```
